32 devices in a mesh: group: 2 (over x), dev: 16 (over z, y, core).
Axes of the slice: x: 2, y: 2, z: 4, core: 2. Of those that a mesh axis runs over, the one named last changes fastest.
Arguments:
- queries: bfloat16 [128, 4096], P(('group', 'dev')), parts along dimension 0, may hold values from -6 to 6
- cache_keys: bfloat16 [128, 512, 256], P(('group', 'dev')), parts along dimension 0, may hold values from -4 to 4
- cache_values: bfloat16 [128, 512, 256], P(('group', 'dev')), parts along dimension 0, may hold values from -6 to 6
- row_lengths: int32 [128], P(('group', 'dev')), parts along dimension 0, may hold values from 2 to 512, as said below
- residual: bfloat16 [128, 7168], P(('group', 'dev')), parts along dimension 0, may hold values from -6 to 6
- out_weight: bfloat16 [16, 1024, 1792], P('dev'), may hold values from -0.3125 to 0.3125
- norm_gain: float32 [7168], replicated, may hold values from 0.1 to 1.9
- expert_ids: int32 [128, 3], P(('group', 'dev')), parts along dimension 0, may hold values from 0 to 3, all different within a row
- gate_scores: float32 [128, 3], P(('group', 'dev')), parts along dimension 0, may hold values from -6 to 6
- gate_weight: bfloat16 [7168, 10240], P(None, 'dev'), may hold values from -0.0625 to 0.0625
- up_weight: bfloat16 [7168, 10240], P(None, 'dev'), may hold values from -0.0625 to 0.0625
- down_weight: bfloat16 [16, 2560, 1792], P('dev'), may hold values from -0.125 to 0.125
Outputs:
- layer_out: bfloat16 [128, 7168], P(('group', 'dev')), parts along dimension 0
The draws below stay inside these ranges and needn't reach their ends.
There are 2 independent parts, one for each index of `group`. The reference program is written for one: setup_inputs(seed, part) draws one part's arguments, and reference() takes and returns one part's arrays. A program takes and returns all parts, laid end to end along the dimension named above; an argument that names none is the same for every part. Nothing has to cross between parts.
Inputs may be any that keep to these rules, and one draw needn't show every extreme that they name: `row_lengths`: each request's cache is live from position 0 up to its length; some request of the part has all 512 positions live.
All inputs are finite; a program needn't handle non-finite values.
Results may differ from the reference program's by a relative error of at most 0.012.
Values may be sent and summed in bfloat16 or wider, within the bound.
A program may use at most 64 MiB of HBM per device.

```python
import jax
import jax.numpy as jnp
from jax import lax

D = 7168
HD = 256
FF = 2560
EXPERTS = 4
TOPK = 3
COLS = 4
CACHE = 512
HEADS = 16
ROWS = 64
KSPLIT = 4
KB = 1024
HB = 2560
DB = 1792


def draw_queries(key, part):
    key = jax.random.fold_in(key, 1)
    drawn = 1.5 * jnp.clip(jax.random.normal(key, (ROWS, HEADS, HD), jnp.float32), -4.0, 4.0)
    return drawn.reshape(ROWS, HEADS * HD).astype(jnp.bfloat16)


def draw_cache_keys(key, part):
    key = jax.random.fold_in(key, 2)
    drawn = jnp.clip(jax.random.normal(key, (ROWS, CACHE, HD), jnp.float32), -4.0, 4.0)
    return drawn.astype(jnp.bfloat16)


def draw_row_lengths(key, part):
    key = jax.random.fold_in(key, 3)
    raw_draw = jax.random.randint(key, (ROWS,), 0, 1024, dtype=jnp.int32)
    lengths = 2 + raw_draw * raw_draw * (CACHE - 2) // (1023 * 1023)
    chosen = jax.random.randint(jax.random.fold_in(key, 5), (), 0, ROWS, dtype=jnp.int32)
    return jnp.where(jnp.arange(ROWS, dtype=jnp.int32) == chosen, CACHE, lengths).astype(jnp.int32)


def level_of(key, extent, pieces, low, high):
    def one(dim, shards_of):
        draws = jax.random.uniform(jax.random.fold_in(jax.random.fold_in(key, 6), dim), (shards_of,), jnp.float32, low / len(pieces), high / len(pieces))
        return jnp.repeat(jnp.exp(draws), extent[dim] // shards_of).reshape((-1,) + (1,) * (len(extent) - dim - 1))

    factor_of = one(*pieces[0])
    for cut in pieces[1:]:
        factor_of = factor_of * one(*cut)
    return factor_of


def distinct(rng, rows, count, top, lift):
    ranking = jax.random.permutation(jax.random.fold_in(rng, 1), count)
    favour = ranking
    for power in range(3):
        favour = favour * favour // count
    favour = favour * lift // count
    chance = jax.random.randint(jax.random.fold_in(rng, 2), (rows, count), 0, 4096) + favour
    sure = jax.random.permutation(jax.random.fold_in(rng, 3), rows)[jnp.arange(count) % rows]
    chance = jnp.where(jnp.arange(rows)[:, None] == sure[None, :], 1 << 14, chance)
    merit = chance * count + jnp.arange(count)
    return lax.top_k(merit.astype(jnp.int32), top)[1].astype(jnp.int32)


def bell_draw(key, extent, spread, bound, shards=(), kind=jnp.bfloat16):
    gain = level_of(key, extent, shards, -0.22, 0.18) if shards else 1.0
    result = jax.random.normal(key, extent, jnp.float32) * spread * gain
    return jnp.minimum(jnp.maximum(result, -bound), bound).astype(kind)


def setup_inputs(seed: int = 0, part: int = 0) -> dict:
    keys = jax.random.split(jax.random.key(seed), 13)
    part_keys = jax.random.split(jax.random.fold_in(keys[12], part), 13)
    queries = draw_queries(jax.random.fold_in(jax.random.fold_in(keys[12], part), 71), part)
    cache_keys = draw_cache_keys(jax.random.fold_in(jax.random.fold_in(keys[12], part), 71), part)
    cache_values = bell_draw(part_keys[2], (ROWS, CACHE, HD), 1.0, 6.0, ((0, 16),))
    row_lengths = draw_row_lengths(jax.random.fold_in(jax.random.fold_in(keys[12], part), 71), part)
    residual = bell_draw(part_keys[4], (ROWS, D), 1.0, 6.0, ((0, 16),))
    out_weight = bell_draw(keys[5], (KSPLIT * COLS, KB, DB), (HEADS * 24) ** -0.5, 0.3125, ((0, 16),))
    norm_gain = jnp.clip(1.0 + 0.18 * jax.random.normal(keys[6], (D,), jnp.float32), 0.1, 1.9)
    expert_ids = distinct(part_keys[7], ROWS, EXPERTS, TOPK, 6144)
    gate_scores = bell_draw(part_keys[8], (ROWS, TOPK), 2.0, 6.0, ((0, 16),), jnp.float32)
    gate_weight = bell_draw(keys[9], (D, EXPERTS * FF), D ** -0.5, 0.0625, ((1, 16),))
    up_weight = bell_draw(keys[10], (D, EXPERTS * FF), D ** -0.5, 0.0625, ((1, 16),))
    down_weight = bell_draw(keys[11], (KSPLIT * COLS, HB, DB), FF ** -0.5, 0.125, ((0, 16),))
    return dict(queries=queries, cache_keys=cache_keys, cache_values=cache_values, row_lengths=row_lengths, residual=residual, out_weight=out_weight, norm_gain=norm_gain, expert_ids=expert_ids, gate_scores=gate_scores, gate_weight=gate_weight, up_weight=up_weight, down_weight=down_weight)


def untile(blocks, row_count, col_count):
    shaped = blocks.reshape(KSPLIT, COLS, blocks.shape[1], blocks.shape[2])
    return jnp.transpose(shaped, (0, 2, 1, 3)).reshape(row_count, col_count)

def reference(queries, cache_keys, cache_values, row_lengths, residual, out_weight, norm_gain, expert_ids, gate_scores, gate_weight, up_weight, down_weight):
    out_matrix = untile(out_weight, HEADS * HD, D)
    down_matrix = untile(down_weight, EXPERTS * FF, D)
    score_scale = HD ** (-0.5)
    query_heads = queries.astype(jnp.float32).reshape(ROWS, HEADS, HD)
    scores = jnp.einsum('rhc,rlc->rhl', query_heads, cache_keys.astype(jnp.float32)) * score_scale
    positions = jnp.arange(CACHE, dtype=jnp.int32)
    is_live = (positions[None, :] < row_lengths[:, None])[:, None, :]
    masked = jnp.where(is_live, scores, -1e+30)
    largest = lax.optimization_barrier(jnp.max(masked, axis=-1, keepdims=True))
    exponent = jnp.where(is_live, jnp.exp(masked - largest), 0.0)
    attn_probs = (exponent / lax.optimization_barrier(jnp.sum(exponent, axis=-1, keepdims=True))).astype(jnp.bfloat16)
    context = jnp.einsum('rhl,rlc->rhc', attn_probs.astype(jnp.float32), cache_values.astype(jnp.float32))
    context = context.astype(jnp.bfloat16).reshape(ROWS, HEADS * HD)
    attended = residual.astype(jnp.float32) + jnp.dot(context, out_matrix, preferred_element_type=jnp.float32)
    mean_square = lax.optimization_barrier(jnp.mean(attended * attended, axis=-1, keepdims=True))
    normed = (attended * lax.rsqrt(mean_square + 1e-05) * norm_gain[None, :]).astype(jnp.bfloat16)
    sigmoid_scores = jax.nn.sigmoid(gate_scores)
    shares = sigmoid_scores / lax.optimization_barrier(jnp.sum(sigmoid_scores, axis=-1, keepdims=True))
    one_hot = (expert_ids[:, :, None] == jnp.arange(EXPERTS, dtype=jnp.int32)[None, None, :]).astype(jnp.float32)
    expert_weight = lax.optimization_barrier(jnp.sum(shares[:, :, None] * one_hot, axis=1)).astype(jnp.bfloat16)
    mixture = jnp.zeros((ROWS, D), jnp.float32)
    for expert in range(EXPERTS):
        gate_act = jnp.dot(normed, gate_weight[:, expert * FF:(expert + 1) * FF], preferred_element_type=jnp.float32)
        up_act = jnp.dot(normed, up_weight[:, expert * FF:(expert + 1) * FF], preferred_element_type=jnp.float32)
        hidden = (jax.nn.silu(gate_act) * up_act).astype(jnp.bfloat16)
        expert_out = jnp.dot(hidden, down_matrix[expert * FF:(expert + 1) * FF, :], preferred_element_type=jnp.float32)
        mixture = mixture + expert_weight[:, expert].astype(jnp.float32)[:, None] * expert_out
    return (attended + mixture).astype(jnp.bfloat16)
```

```python
import functools

import jax
import jax.numpy as jnp
from jax import lax
from jax.experimental import pallas as pl
from jax.experimental.pallas import tpu as pltpu
from jax.sharding import PartitionSpec as P

EXPERTS = 4
COLS = 4
LANES = 128
F32 = jnp.float32
BF16 = jnp.bfloat16


def dot(a, b):
    return jnp.dot(a, b, preferred_element_type=F32)


def kernel(
    n,
    q_ref,
    len_ref,
    res_ref,
    gain_ref,
    ids_ref,
    score_ref,
    keys_hbm,
    values_hbm,
    wo_hbm,
    wg_hbm,
    wu_hbm,
    wd_hbm,
    out_ref,
    keys,
    values,
    wo,
    wg,
    wu,
    wd,
    q_rows,
    ctx_send,
    ctx_recv,
    ctx_all,
    mix_send,
    mix_recv,
    mix_all,
    res_recv,
    part,
    part_send,
    part_recv,
    attended,
    y_all,
    hid_all,
    acc,
    fin_send,
    fin_recv,
    kv_sem,
    w_sem,
    ctx_ssem,
    ctx_rsem,
    mix_ssem,
    mix_rsem,
    res_ssem,
    res_rsem,
    part_ssem,
    part_rsem,
    z_ssem,
    z_rsem,
    y_ssem,
    y_rsem,
    c_ssem,
    c_rsem,
    hid_ssem,
    hid_rsem,
    fin_ssem,
    fin_rsem,
):
    me = lax.axis_index("dev")
    splits = n // COLS
    k = me // COLS
    c = lax.rem(me, COLS)
    rows = q_ref.shape[0]
    head_dim = keys.shape[2]
    cache_len = keys.shape[1]
    heads = q_ref.shape[1] // head_dim
    per_block = heads // splits
    kb = wo.shape[0]
    db = wo.shape[1]
    ff = wg.shape[1]
    blk = rows * COLS
    all_rows = rows * n
    width = db * COLS

    def remote(src, dst, ssem, rsem, dev):
        return pltpu.make_async_remote_copy(
            src_ref=src,
            dst_ref=dst,
            send_sem=ssem,
            recv_sem=rsem,
            device_id={"dev": dev},
            device_id_type=pl.DeviceIdType.MESH,
        )

    loads = []
    for r in range(rows):
        loads.append(pltpu.make_async_copy(keys_hbm.at[r], keys.at[r], kv_sem.at[r]))
    for r in range(rows):
        loads.append(pltpu.make_async_copy(values_hbm.at[r], values.at[r], kv_sem.at[rows + r]))
    for copy in loads:
        copy.start()
    load_o = pltpu.make_async_copy(wo_hbm.at[0], wo, w_sem.at[0])

    def xor(a, bit):
        return a + bit - 2 * bit * lax.rem(a // bit, 2)

    beside = xor(c, 1)
    across = xor(c, 2)
    corner = xor(beside, 2)

    def plane(i):
        return (c, beside, across, corner)[i]

    def w_slice(i):
        return pl.ds(pl.multiple_of(plane(i) * db, db), db)

    load_g = [
        pltpu.make_async_copy(wg_hbm.at[w_slice(i)], wg.at[w_slice(i)], w_sem.at[1 + i])
        for i in range(COLS)
    ]
    load_u = [
        pltpu.make_async_copy(wu_hbm.at[w_slice(i)], wu.at[w_slice(i)], w_sem.at[5 + i])
        for i in range(COLS)
    ]

    def d_slice(i):
        return pl.ds(pl.multiple_of(plane(i) * ff, ff), ff)

    load_d = [
        pltpu.make_async_copy(wd_hbm.at[0, d_slice(i)], wd.at[d_slice(i)], w_sem.at[9 + i])
        for i in range(COLS)
    ]

    barrier = pltpu.get_barrier_semaphore()

    def greet(i, carry):
        pl.semaphore_signal(
            barrier,
            inc=1,
            device_id={"dev": lax.rem(me + i, n)},
            device_id_type=pl.DeviceIdType.MESH,
        )
        return carry

    lax.fori_loop(1, n, greet, 0)
    load_o.start()
    for i in range(COLS):
        load_g[i].start()
        load_u[i].start()
    for i in range(COLS):
        load_d[i].start()

    shares = 1.0 / (1.0 + jnp.exp(-score_ref[...]))
    total = jnp.sum(shares, axis=-1, keepdims=True)
    lane = lax.broadcasted_iota(jnp.int32, (rows, LANES), 1)
    mine = jnp.zeros((rows, LANES), F32)
    for t in range(ids_ref.shape[1]):
        share = shares[:, t : t + 1] / total
        mine = mine + jnp.where(ids_ref[:, t : t + 1] == lane, share, 0.0)
    mix_send[...] = mine.astype(BF16).astype(F32)

    for h in range(heads):
        q_rows[h * rows : (h + 1) * rows, :] = q_ref[:, h * head_dim : (h + 1) * head_dim].astype(
            F32
        )
    qs = q_rows[...].astype(BF16)
    hr = heads * rows
    which = lax.rem(lax.broadcasted_iota(jnp.int32, (hr, 1), 0), rows)
    scores = jnp.zeros((hr, cache_len), F32)
    lengths = jnp.zeros((hr, 1), jnp.int32)
    for r in range(rows):
        loads[r].wait()
        s = lax.dot_general(qs, keys[r], (((1,), (1,)), ((), ())), preferred_element_type=F32)
        scores = jnp.where(which == r, s, scores)
        lengths = jnp.where(which == r, len_ref[r], lengths)
    live = lax.broadcasted_iota(jnp.int32, (hr, cache_len), 1) < lengths
    scores = jnp.where(live, scores * head_dim ** (-0.5), -1e30)
    largest = jnp.max(scores, axis=-1, keepdims=True)
    exponent = jnp.where(live, jnp.exp(scores - largest), 0.0)
    probs = exponent / jnp.sum(exponent, axis=-1, keepdims=True)
    context = jnp.zeros((hr, head_dim), F32)
    for r in range(rows):
        loads[rows + r].wait()
        context = context + dot(jnp.where(which == r, probs, 0.0).astype(BF16), values[r])
    for h in range(heads):
        b, at = h // per_block, h % per_block
        ctx_send[b, :, at * head_dim : (at + 1) * head_dim] = context[
            h * rows : (h + 1) * rows, :
        ].astype(BF16)

    pl.semaphore_wait(barrier, n - 1)

    def ctx_copy(i):
        to = lax.rem(me + i, n)
        return remote(
            ctx_send.at[to // COLS], ctx_recv.at[me], ctx_ssem.at[i], ctx_rsem.at[i], to
        )

    def mix_copy(i):
        to = lax.rem(me + i, n)
        return remote(mix_send, mix_recv.at[me], mix_ssem.at[i], mix_rsem.at[i], to)

    def res_copy(i):
        to = lax.rem(c + i, COLS)
        cols = pl.ds(pl.multiple_of(to * db, LANES), db)
        return remote(
            res_ref.at[:, cols], res_recv.at[c], res_ssem.at[i], res_rsem.at[i], k * COLS + to
        )

    def loop(low, high, f):
        def step(i, carry):
            f(i)
            return carry

        lax.fori_loop(low, high, step, 0)

    loop(1, n, lambda i: ctx_copy(i).start())
    loop(1, COLS, lambda i: res_copy(i).start())
    loop(1, n, lambda i: mix_copy(i).start())
    ctx_recv[me] = ctx_send[k]
    mix_recv[me] = mix_send[...]
    res_recv[c] = res_ref[:, pl.ds(pl.multiple_of(c * db, LANES), db)]
    load_o.wait()
    loop(1, n, lambda i: ctx_copy(i).wait_recv())
    for d in range(n):
        ctx_all[d * rows : (d + 1) * rows, :] = ctx_recv[d].astype(F32)
    part[...] = dot(ctx_all[...].astype(BF16), wo[...])

    for b in range(splits):
        part_send[b] = part[b * blk : (b + 1) * blk, :].astype(BF16)

    def part_copy(i):
        to = lax.rem(k + i, splits)
        return remote(
            part_send.at[to], part_recv.at[i], part_ssem.at[i], part_rsem.at[i], to * COLS + c
        )

    loop(1, splits, lambda i: part_copy(i).start())
    loop(1, COLS, lambda i: res_copy(i).wait_recv())
    for j in range(COLS):
        attended[j * rows : (j + 1) * rows, :] = res_recv[j].astype(F32)
    mine_rows = pl.ds(pl.multiple_of(k * blk, blk), blk)
    total = attended[...] + part[mine_rows, :]
    gain = gain_ref[:, pl.ds(pl.multiple_of(c * db, LANES), db)]
    for i in range(1, splits):
        part_copy(i).wait_recv()
        total = total + part_recv[i].astype(F32)
    attended[...] = total
    square = jnp.sum(total * total, axis=-1, keepdims=True)
    high = square.astype(BF16).astype(F32)
    lane = lax.broadcasted_iota(jnp.int32, (blk, LANES), 1)
    packed = jnp.where(lane == 0, high, jnp.where(lane == 1, square - high, 0.0))
    y_all[c, mine_rows, 0:db] = (total * gain).astype(BF16)
    y_all[c, mine_rows, db : db + LANES] = packed.astype(BF16)

    def piece(col, i):
        from_k = lax.rem(k + splits - i, splits)
        return y_all.at[col, pl.ds(pl.multiple_of(from_k * blk, blk), blk)]

    def z_copy(i):
        to = lax.rem(k + i, splits)
        return remote(piece(c, 0), piece(c, 0), z_ssem.at[i], z_rsem.at[i], to * COLS + c)

    def y_copy(i):
        return remote(
            piece(c, i), piece(c, i), y_ssem.at[i], y_rsem.at[i], k * COLS + across
        )

    def c_copy(col, base, i):
        return remote(
            piece(col, i),
            piece(col, i),
            c_ssem.at[base + i],
            c_rsem.at[base + i],
            k * COLS + beside,
        )

    loop(1, splits, lambda i: z_copy(i).start())
    y_copy(0).start()
    c_copy(c, 0, 0).start()

    def forward_z(i):
        z_copy(i).wait_recv()
        y_copy(i).start()
        c_copy(c, 0, i).start()

    def forward_y(i):
        y_copy(i).wait_recv()
        c_copy(across, splits, i).start()

    loop(1, splits, forward_z)

    def chunk(i, col):
        load_g[i].wait()
        load_u[i].wait()
        lhs = y_all[col, :, 0:db]
        at = pl.ds(pl.multiple_of(col * db, db), db)
        tail = y_all[col, :, db : db + LANES].astype(F32)
        return dot(lhs, wg[at, :]), dot(lhs, wu[at, :]), jnp.sum(tail, axis=-1, keepdims=True)

    gate, up, square = chunk(0, c)
    loop(0, splits, forward_y)
    loop(0, splits, lambda i: c_copy(beside, 0, i).wait_recv())
    g, u, s = chunk(1, beside)
    gate, up, square = gate + g, up + u, square + s
    g, u, s = chunk(2, across)
    gate, up, square = gate + g, up + u, square + s
    loop(0, splits, lambda i: c_copy(corner, splits, i).wait_recv())
    g, u, s = chunk(3, corner)
    gate, up, square = gate + g, up + u, square + s
    scale = lax.rsqrt(square * (1.0 / width) + 1e-5)
    gate = gate * scale
    hidden = gate / (1.0 + jnp.exp(-gate)) * (up * scale)
    hid_all[c] = hidden.astype(BF16)

    def hid_copy(i):
        return remote(
            hid_all.at[c], hid_all.at[c], hid_ssem.at[i], hid_rsem.at[i], k * COLS + plane(i)
        )

    for i in (2, 3, 1):
        hid_copy(i).start()
    loop(1, n, lambda i: mix_copy(i).wait_recv())
    for d in range(n):
        mix_all[d * rows : (d + 1) * rows, :] = mix_recv[d]
    lane = lax.broadcasted_iota(jnp.int32, (all_rows, LANES), 1)
    expert = k // (splits // EXPERTS)
    weight = jnp.sum(jnp.where(lane == expert, mix_all[...], 0.0), axis=-1, keepdims=True)
    for i in range(COLS):
        load_d[i].wait()
        if i:
            hid_copy(i).wait_recv()
        at = pl.ds(pl.multiple_of(plane(i) * ff, ff), ff)
        term = dot(hid_all[plane(i)], wd[at, :])
        acc[...] = term if i == 0 else acc[...] + term
    acc[...] = acc[...] * weight
    acc[mine_rows, :] = acc[mine_rows, :] + attended[...]
    for d in range(n):
        fin_send[d] = acc[d * rows : (d + 1) * rows, :].astype(BF16)

    def fin_copy(i):
        to = lax.rem(me + i, n)
        return remote(fin_send.at[to], fin_recv.at[me], fin_ssem.at[i], fin_rsem.at[i], to)

    loop(1, n, lambda i: fin_copy(i).start())
    fin_recv[me] = fin_send[me]
    loop(1, n, lambda i: fin_copy(i).wait_recv())
    for j in range(COLS):
        total = fin_recv[j].astype(F32)
        for b in range(1, splits):
            total = total + fin_recv[b * COLS + j].astype(F32)
        out_ref[:, j * db : (j + 1) * db] = total.astype(BF16)

    def drain(i):
        ctx_copy(i).wait_send()
        mix_copy(i).wait_send()
        fin_copy(i).wait_send()

    loop(1, n, drain)

    def drain_split(i):
        part_copy(i).wait_send()
        z_copy(i).wait_send()

    loop(1, splits, drain_split)

    def drain_plane(i):
        y_copy(i).wait_send()
        c_copy(c, 0, i).wait_send()
        c_copy(across, splits, i).wait_send()

    loop(0, splits, drain_plane)
    for i in range(1, COLS):
        res_copy(i).wait_send()
        hid_copy(i).wait_send()


def body(
    queries,
    cache_keys,
    cache_values,
    row_lengths,
    residual,
    out_weight,
    norm_gain,
    expert_ids,
    gate_scores,
    gate_weight,
    up_weight,
    down_weight,
):
    n = lax.axis_size("dev")
    splits = n // COLS
    rows = queries.shape[0]
    head_dim = cache_keys.shape[2]
    heads = queries.shape[1] // head_dim
    kb, db = out_weight.shape[1:]
    ff = gate_weight.shape[1]
    all_rows = rows * n
    blk = rows * COLS
    vmem = pl.BlockSpec(memory_space=pltpu.VMEM)
    hbm = pl.BlockSpec(memory_space=pl.ANY)
    smem = pl.BlockSpec(memory_space=pltpu.SMEM)

    def dma(*count):
        return pltpu.SemaphoreType.DMA(count)

    return pl.pallas_call(
        functools.partial(kernel, n),
        out_shape=jax.ShapeDtypeStruct(residual.shape, BF16),
        in_specs=[vmem, smem, vmem, vmem, vmem, vmem] + [hbm] * 6,
        out_specs=vmem,
        scratch_shapes=[
            pltpu.VMEM(cache_keys.shape, BF16),
            pltpu.VMEM(cache_values.shape, BF16),
            pltpu.VMEM((kb, db), BF16),
            pltpu.VMEM(gate_weight.shape, BF16),
            pltpu.VMEM(up_weight.shape, BF16),
            pltpu.VMEM(down_weight.shape[1:], BF16),
            pltpu.VMEM((heads * rows, head_dim), F32),
            pltpu.VMEM((splits, rows, kb), BF16),
            pltpu.VMEM((n, rows, kb), BF16),
            pltpu.VMEM((all_rows, kb), F32),
            pltpu.VMEM((rows, LANES), F32),
            pltpu.VMEM((n, rows, LANES), F32),
            pltpu.VMEM((all_rows, LANES), F32),
            pltpu.VMEM((COLS, rows, db), BF16),
            pltpu.VMEM((all_rows, db), F32),
            pltpu.VMEM((splits, blk, db), BF16),
            pltpu.VMEM((splits, blk, db), BF16),
            pltpu.VMEM((blk, db), F32),
            pltpu.VMEM((COLS, all_rows, db + LANES), BF16),
            pltpu.VMEM((COLS, all_rows, ff), BF16),
            pltpu.VMEM((all_rows, db), F32),
            pltpu.VMEM((n, rows, db), BF16),
            pltpu.VMEM((n, rows, db), BF16),
            dma(2 * rows),
            dma(13),
            dma(n),
            dma(n),
            dma(n),
            dma(n),
            dma(COLS),
            dma(COLS),
            dma(splits),
            dma(splits),
            dma(splits),
            dma(splits),
            dma(splits),
            dma(splits),
            dma(2 * splits),
            dma(2 * splits),
            dma(COLS),
            dma(COLS),
            dma(n),
            dma(n),
        ],
        compiler_params=pltpu.CompilerParams(
            collective_id=0, has_side_effects=True, vmem_limit_bytes=60 * 1024 * 1024
        ),
        name="layer",
    )(
        queries,
        row_lengths,
        residual,
        norm_gain[None, :],
        expert_ids,
        gate_scores,
        cache_keys,
        cache_values,
        out_weight,
        gate_weight,
        up_weight,
        down_weight,
    )


def solution(mesh):
    return jax.shard_map(
        body,
        mesh=mesh,
        in_specs=(
            P(("group", "dev"), None),
            P(("group", "dev"), None, None),
            P(("group", "dev"), None, None),
            P(("group", "dev")),
            P(("group", "dev"), None),
            P("dev", None, None),
            P(),
            P(("group", "dev"), None),
            P(("group", "dev"), None),
            P(None, "dev"),
            P(None, "dev"),
            P("dev", None, None),
        ),
        out_specs=P(("group", "dev"), None),
        check_vma=False,
    )
```

```python
import functools

import jax
import jax.numpy as jnp
from jax import lax
from jax.experimental import pallas as pl
from jax.experimental.pallas import tpu as pltpu
from jax.sharding import PartitionSpec as P

EXPERTS = 4
COLS = 4
LANES = 128
HALVES = 2
F32 = jnp.float32
BF16 = jnp.bfloat16


def dot(a, b):
    return jnp.dot(a, b, preferred_element_type=F32)


def kernel(
    n,
    q_hbm,
    len_hbm,
    res_hbm,
    gain_hbm,
    ids_hbm,
    score_hbm,
    keys_hbm,
    values_hbm,
    wo_hbm,
    wg_hbm,
    wu_hbm,
    wd_hbm,
    out_ref,
    q_ref,
    len_ref,
    res_ref,
    gain_ref,
    ids_ref,
    score_ref,
    keys,
    values,
    wo,
    wg,
    wu,
    wd,
    q_rows,
    ctx_send,
    ctx_recv,
    ctx_all,
    res_send,
    res_recv,
    extra,
    part,
    part_send,
    part_recv,
    attended,
    y_first,
    y_second,
    hid_all,
    acc,
    fin_send,
    fin_recv,
    in_sem,
    kv_sem,
    w_sem,
    ctx_ssem,
    ctx_rsem,
    res_ssem,
    res_rsem,
    part_ssem,
    part_rsem,
    z_ssem,
    z_rsem,
    y_ssem,
    y_rsem,
    c_ssem,
    c_rsem,
    hid_ssem,
    hid_rsem,
    fin_ssem,
    fin_rsem,
):
    me = lax.axis_index("dev")
    splits = n // COLS
    k = me // COLS
    c = lax.rem(me, COLS)
    rows = q_ref.shape[0]
    head_dim = keys.shape[2]
    cache_len = keys.shape[1]
    heads = q_ref.shape[1] // head_dim
    per_block = heads // splits
    db = wo.shape[1]
    half = db // HALVES
    ff = wg.shape[1]
    blk = rows * COLS
    all_rows = rows * n
    width = db * COLS
    y_all = (y_first, y_second)

    barrier = pltpu.get_barrier_semaphore()

    def loop(low, high, f):
        def step(i, carry):
            f(i)
            return carry

        lax.fori_loop(low, high, step, 0)

    def greet(i):
        pl.semaphore_signal(
            barrier,
            inc=1,
            device_id={"dev": lax.rem(me + i, n)},
            device_id_type=pl.DeviceIdType.MESH,
        )

    loop(1, n, greet)

    def remote(src, dst, ssem, rsem, dev):
        return pltpu.make_async_remote_copy(
            src_ref=src,
            dst_ref=dst,
            send_sem=ssem,
            recv_sem=rsem,
            device_id={"dev": dev},
            device_id_type=pl.DeviceIdType.MESH,
        )

    def xor(a, bits):
        bit = 1
        while bit <= bits:
            if bits & bit:
                a = a + bit - 2 * bit * lax.rem(a // bit, 2)
            bit *= 2
        return a

    beside = xor(c, 1)
    across = xor(c, 2)
    corner = xor(c, 3)
    plane = (c, beside, across, corner)

    small = [
        pltpu.make_async_copy(src, dst, in_sem.at[i])
        for i, (src, dst) in enumerate(
            (
                (q_hbm, q_ref),
                (len_hbm, len_ref),
                (res_hbm, res_ref),
                (gain_hbm, gain_ref),
                (ids_hbm, ids_ref),
                (score_hbm, score_ref),
            )
        )
    ]
    loads = [pltpu.make_async_copy(keys_hbm.at[r], keys.at[r], kv_sem.at[r]) for r in range(rows)]
    loads += [
        pltpu.make_async_copy(values_hbm.at[r], values.at[r], kv_sem.at[rows + r])
        for r in range(rows)
    ]
    load_o = pltpu.make_async_copy(wo_hbm.at[0], wo, w_sem.at[0])

    def span(i, size):
        return pl.ds(pl.multiple_of(plane[i] * size, size), size)

    load_g = [
        pltpu.make_async_copy(wg_hbm.at[span(i, db)], wg.at[span(i, db)], w_sem.at[1 + i])
        for i in range(COLS)
    ]
    load_u = [
        pltpu.make_async_copy(wu_hbm.at[span(i, db)], wu.at[span(i, db)], w_sem.at[5 + i])
        for i in range(COLS)
    ]
    load_d = [
        pltpu.make_async_copy(wd_hbm.at[0, span(i, ff)], wd.at[span(i, ff)], w_sem.at[9 + i])
        for i in range(COLS)
    ]
    small[0].start()
    small[1].start()
    for copy in loads:
        copy.start()
    for copy in small[2:]:
        copy.start()
    load_o.start()
    for i in range(COLS):
        load_g[i].start()
        load_u[i].start()
    for i in range(COLS):
        load_d[i].start()

    small[0].wait()
    small[1].wait()
    for h in range(heads):
        q_rows[h * rows : (h + 1) * rows, :] = q_ref[:, h * head_dim : (h + 1) * head_dim].astype(
            F32
        )
    qs = q_rows[...].astype(BF16)
    hr = heads * rows
    which = lax.rem(lax.broadcasted_iota(jnp.int32, (hr, 1), 0), rows)
    scores = jnp.zeros((hr, cache_len), F32)
    lengths = jnp.zeros((hr, 1), jnp.int32)
    for r in range(rows):
        loads[r].wait()
        s = lax.dot_general(qs, keys[r], (((1,), (1,)), ((), ())), preferred_element_type=F32)
        scores = jnp.where(which == r, s, scores)
        lengths = jnp.where(which == r, len_ref[r], lengths)
    live = lax.broadcasted_iota(jnp.int32, (hr, cache_len), 1) < lengths
    scores = jnp.where(live, scores * head_dim ** (-0.5), -1e30)
    largest = jnp.max(scores, axis=-1, keepdims=True)
    exponent = jnp.where(live, jnp.exp(scores - largest), 0.0)
    probs = exponent / jnp.sum(exponent, axis=-1, keepdims=True)
    context = jnp.zeros((hr, head_dim), F32)
    for r in range(rows):
        loads[rows + r].wait()
        context = context + dot(jnp.where(which == r, probs, 0.0).astype(BF16), values[r])
    for h in range(heads):
        b, at = h // per_block, h % per_block
        ctx_send[b, :, at * head_dim : (at + 1) * head_dim] = context[
            h * rows : (h + 1) * rows, :
        ].astype(BF16)

    for copy in small[2:]:
        copy.wait()
    shares = 1.0 / (1.0 + jnp.exp(-score_ref[...]))
    total = jnp.sum(shares, axis=-1, keepdims=True)
    lane = lax.broadcasted_iota(jnp.int32, (rows, LANES), 1)
    mine = jnp.zeros((rows, LANES), F32)
    for t in range(ids_ref.shape[1]):
        share = shares[:, t : t + 1] / total
        mine = mine + jnp.where(ids_ref[:, t : t + 1] + 2 == lane, share, 0.0)
    for j in range(COLS):
        res_send[j, :, 0:db] = res_ref[:, j * db : (j + 1) * db]
        res_send[j, :, db : db + LANES] = mine.astype(BF16)
    res_recv[c] = res_send[c]
    ctx_recv[me] = ctx_send[k]

    def ctx_copy(i):
        to = lax.rem(me + i, n)
        return remote(
            ctx_send.at[to // COLS], ctx_recv.at[me], ctx_ssem.at[i], ctx_rsem.at[i], to
        )

    def res_copy(i):
        to = lax.rem(c + i, COLS)
        return remote(
            res_send.at[to], res_recv.at[c], res_ssem.at[i], res_rsem.at[i], k * COLS + to
        )

    def part_copy(h, i):
        to = xor(k, i)
        return remote(
            part_send.at[h, to],
            part_recv.at[h, i],
            part_ssem.at[h, i],
            part_rsem.at[h, i],
            to * COLS + c,
        )

    pl.semaphore_wait(barrier, n - 1)
    loop(1, n, lambda i: ctx_copy(i).start())
    load_o.wait()
    loop(1, n, lambda i: ctx_copy(i).wait_recv())
    for d in range(n):
        ctx_all[d * rows : (d + 1) * rows, :] = ctx_recv[d].astype(F32)
    lhs = ctx_all[...].astype(BF16)

    for h in range(HALVES):
        cols = slice(h * half, (h + 1) * half)
        part[:, cols] = dot(lhs, wo[:, cols])
        for b in range(splits):
            part_send[h, b] = part[b * blk : (b + 1) * blk, cols].astype(BF16)
        for i in range(1, splits):
            part_copy(h, i).start()
        if h == 0:
            loop(1, COLS, lambda i: res_copy(i).start())

    loop(1, COLS, lambda i: res_copy(i).wait_recv())
    for j in range(COLS):
        attended[j * rows : (j + 1) * rows, :] = res_recv[j, :, 0:db].astype(F32)
        extra[j * rows : (j + 1) * rows, :] = res_recv[j, :, db : db + LANES].astype(F32)
    mine_rows = pl.ds(pl.multiple_of(k * blk, blk), blk)

    def piece(h, col, i):
        return y_all[h].at[col, pl.ds(pl.multiple_of(xor(k, i) * blk, blk), blk)]

    def z_copy(h, i):
        at = piece(h, c, 0)
        return remote(at, at, z_ssem.at[h, i], z_rsem.at[h, i], xor(k, i) * COLS + c)

    def y_copy(h, i):
        at = piece(h, c, i)
        return remote(at, at, y_ssem.at[h, i], y_rsem.at[h, i], k * COLS + across)

    def c_copy(h, far, i):
        at = piece(h, across if far else c, i)
        slot = splits * far + i
        return remote(at, at, c_ssem.at[h, slot], c_rsem.at[h, slot], k * COLS + beside)

    square = jnp.zeros((blk, 1), F32)
    for h in range(HALVES):
        cols = slice(h * half, (h + 1) * half)
        total = attended[:, cols] + part[mine_rows, cols]
        for i in range(1, splits):
            part_copy(h, i).wait_recv()
            total = total + part_recv[h, i].astype(F32)
        attended[:, cols] = total
        gain = gain_ref[:, pl.ds(pl.multiple_of(c * db + h * half, LANES), half)]
        square = square + jnp.sum(total * total, axis=-1, keepdims=True)
        y_all[h][c, mine_rows, 0:half] = (total * gain).astype(BF16)
        if h == HALVES - 1:
            high = square.astype(BF16).astype(F32)
            lane = lax.broadcasted_iota(jnp.int32, (blk, LANES), 1)
            packed = jnp.where(lane == 0, high, jnp.where(lane == 1, square - high, extra[...]))
            y_all[h][c, mine_rows, half : half + LANES] = packed.astype(BF16)
        for i in range(1, splits):
            z_copy(h, i).start()
        y_copy(h, 0).start()
        c_copy(h, 0, 0).start()

    def forward_z(h, i):
        z_copy(h, i).wait_recv()
        y_copy(h, i).start()
        c_copy(h, 0, i).start()

    def forward_y(h, i):
        y_copy(h, i).wait_recv()
        c_copy(h, 1, i).start()

    def chunk(h, i):
        if h == 0:
            load_g[i].wait()
            load_u[i].wait()
        lhs = y_all[h][plane[i], :, 0:half]
        at = pl.ds(pl.multiple_of(plane[i] * db + h * half, half), half)
        return dot(lhs, wg[at, :]), dot(lhs, wu[at, :])

    def arrive(h, far):
        for i in range(splits):
            c_copy(h, far, i).wait_recv()

    for i in range(1, splits):
        forward_z(0, i)
    gate, up = chunk(0, 0)
    forward_y(0, 0)
    for i in range(1, splits):
        forward_z(1, i)
        forward_y(0, i)
    arrive(0, 0)
    for h, i in ((0, 1), (1, 0), (0, 2)):
        g, u = chunk(h, i)
        gate, up = gate + g, up + u
    for i in range(splits):
        forward_y(1, i)
    arrive(0, 1)
    g, u = chunk(0, 3)
    gate, up = gate + g, up + u
    arrive(1, 0)
    for i in (1, 2):
        g, u = chunk(1, i)
        gate, up = gate + g, up + u
    arrive(1, 1)
    g, u = chunk(1, 3)
    gate, up = gate + g, up + u
    lane = lax.broadcasted_iota(jnp.int32, (all_rows, LANES), 1)
    square = jnp.zeros((all_rows, 1), F32)
    for j in range(COLS):
        tail = y_second[j, :, half : half + LANES].astype(F32)
        square = square + jnp.sum(jnp.where(lane < 2, tail, 0.0), axis=-1, keepdims=True)
    expert = k // (splits // EXPERTS)
    weight = jnp.sum(jnp.where(lane == expert + 2, tail, 0.0), axis=-1, keepdims=True)
    scale = lax.rsqrt(square * (1.0 / width) + 1e-5)
    gate = gate * scale
    hidden = gate / (1.0 + jnp.exp(-gate)) * (up * scale)
    hid_all[c] = hidden.astype(BF16)

    def hid_copy(i):
        at = hid_all.at[across if i == 3 else c]
        to = across if i == 2 else beside
        return remote(at, at, hid_ssem.at[i], hid_rsem.at[i], k * COLS + to)

    hid_copy(2).start()
    hid_copy(1).start()
    load_d[0].wait()
    acc[...] = dot(hid_all[c], wd[span(0, ff), :])
    load_d[1].wait()
    hid_copy(1).wait_recv()
    acc[...] += dot(hid_all[beside], wd[span(1, ff), :])
    hid_copy(2).wait_recv()
    hid_copy(3).start()
    load_d[2].wait()
    acc[...] += dot(hid_all[across], wd[span(2, ff), :])
    load_d[3].wait()
    hid_copy(3).wait_recv()

    def fin_copy(h, i):
        to = lax.rem(me + i, n)
        return remote(
            fin_send.at[h, to], fin_recv.at[h, me], fin_ssem.at[h, i], fin_rsem.at[h, i], to
        )

    for h in range(HALVES):
        cols = slice(h * half, (h + 1) * half)
        acc[:, cols] = (acc[:, cols] + dot(hid_all[corner], wd[span(3, ff), cols])) * weight
        acc[mine_rows, cols] = acc[mine_rows, cols] + attended[:, cols]
        for d in range(n):
            fin_send[h, d] = acc[d * rows : (d + 1) * rows, cols].astype(BF16)
        loop(1, n, lambda i: fin_copy(h, i).start())
        fin_recv[h, me] = fin_send[h, me]
    for h in range(HALVES):
        loop(1, n, lambda i: fin_copy(h, i).wait_recv())
        for j in range(COLS):
            total = fin_recv[h, j].astype(F32)
            for b in range(1, splits):
                total = total + fin_recv[h, b * COLS + j].astype(F32)
            out_ref[:, j * db + h * half : j * db + (h + 1) * half] = total.astype(BF16)

    loop(1, n, lambda i: ctx_copy(i).wait_send())
    loop(1, COLS, lambda i: res_copy(i).wait_send())
    for i in range(1, COLS):
        hid_copy(i).wait_send()
    for h in range(HALVES):
        loop(1, n, lambda i: fin_copy(h, i).wait_send())
        for i in range(splits):
            if i:
                part_copy(h, i).wait_send()
                z_copy(h, i).wait_send()
            y_copy(h, i).wait_send()
            c_copy(h, 0, i).wait_send()
            c_copy(h, 1, i).wait_send()


def body(
    queries,
    cache_keys,
    cache_values,
    row_lengths,
    residual,
    out_weight,
    norm_gain,
    expert_ids,
    gate_scores,
    gate_weight,
    up_weight,
    down_weight,
):
    n = lax.axis_size("dev")
    splits = n // COLS
    rows = queries.shape[0]
    head_dim = cache_keys.shape[2]
    heads = queries.shape[1] // head_dim
    kb, db = out_weight.shape[1:]
    ff = gate_weight.shape[1]
    all_rows = rows * n
    blk = rows * COLS
    half = db // HALVES
    vmem = pl.BlockSpec(memory_space=pltpu.VMEM)
    hbm = pl.BlockSpec(memory_space=pltpu.HBM)

    def dma(*count):
        return pltpu.SemaphoreType.DMA(count)

    return pl.pallas_call(
        functools.partial(kernel, n),
        out_shape=jax.ShapeDtypeStruct(residual.shape, BF16),
        in_specs=[hbm] * 12,
        out_specs=vmem,
        scratch_shapes=[
            pltpu.VMEM(queries.shape, BF16),
            pltpu.SMEM(row_lengths.shape, jnp.int32),
            pltpu.VMEM(residual.shape, BF16),
            pltpu.VMEM((1, norm_gain.shape[0]), F32),
            pltpu.VMEM(expert_ids.shape, jnp.int32),
            pltpu.VMEM(gate_scores.shape, F32),
            pltpu.VMEM(cache_keys.shape, BF16),
            pltpu.VMEM(cache_values.shape, BF16),
            pltpu.VMEM((kb, db), BF16),
            pltpu.VMEM(gate_weight.shape, BF16),
            pltpu.VMEM(up_weight.shape, BF16),
            pltpu.VMEM(down_weight.shape[1:], BF16),
            pltpu.VMEM((heads * rows, head_dim), F32),
            pltpu.VMEM((splits, rows, kb), BF16),
            pltpu.VMEM((n, rows, kb), BF16),
            pltpu.VMEM((all_rows, kb), F32),
            pltpu.VMEM((COLS, rows, db + LANES), BF16),
            pltpu.VMEM((COLS, rows, db + LANES), BF16),
            pltpu.VMEM((blk, LANES), F32),
            pltpu.VMEM((all_rows, db), F32),
            pltpu.VMEM((HALVES, splits, blk, half), BF16),
            pltpu.VMEM((HALVES, splits, blk, half), BF16),
            pltpu.VMEM((blk, db), F32),
            pltpu.VMEM((COLS, all_rows, half), BF16),
            pltpu.VMEM((COLS, all_rows, half + LANES), BF16),
            pltpu.VMEM((COLS, all_rows, ff), BF16),
            pltpu.VMEM((all_rows, db), F32),
            pltpu.VMEM((HALVES, n, rows, half), BF16),
            pltpu.VMEM((HALVES, n, rows, half), BF16),
            dma(6),
            dma(2 * rows),
            dma(13),
            dma(n),
            dma(n),
            dma(COLS),
            dma(COLS),
        ]
        + [dma(HALVES, splits)] * 6
        + [dma(HALVES, 2 * splits)] * 2
        + [dma(COLS)] * 2
        + [dma(HALVES, n)] * 2,
        compiler_params=pltpu.CompilerParams(
            collective_id=0, has_side_effects=True, vmem_limit_bytes=60 * 1024 * 1024
        ),
        name="layer",
    )(
        queries,
        row_lengths,
        residual,
        norm_gain[None, :],
        expert_ids,
        gate_scores,
        cache_keys,
        cache_values,
        out_weight,
        gate_weight,
        up_weight,
        down_weight,
    )


def solution(mesh):
    return jax.shard_map(
        body,
        mesh=mesh,
        in_specs=(
            P(("group", "dev"), None),
            P(("group", "dev"), None, None),
            P(("group", "dev"), None, None),
            P(("group", "dev")),
            P(("group", "dev"), None),
            P("dev", None, None),
            P(),
            P(("group", "dev"), None),
            P(("group", "dev"), None),
            P(None, "dev"),
            P(None, "dev"),
            P("dev", None, None),
        ),
        out_specs=P(("group", "dev"), None),
        check_vma=False,
    )
```

```python
import functools

import jax
import jax.numpy as jnp
from jax import lax
from jax.experimental import pallas as pl
from jax.experimental.pallas import tpu as pltpu
from jax.sharding import PartitionSpec as P

EXPERTS = 4
COLS = 4
LANES = 128
HALVES = 2
F32 = jnp.float32
BF16 = jnp.bfloat16


def dot(a, b):
    return jnp.dot(a, b, preferred_element_type=F32)


def kernel(
    n,
    q_hbm,
    len_hbm,
    res_hbm,
    gain_hbm,
    ids_hbm,
    score_hbm,
    keys_hbm,
    values_hbm,
    wo_hbm,
    wg_hbm,
    wu_hbm,
    wd_hbm,
    out_ref,
    q_ref,
    len_ref,
    res_ref,
    gain_ref,
    ids_ref,
    score_ref,
    keys,
    values,
    wo,
    wg,
    wu,
    wd,
    q_rows,
    ctx_send,
    ctx_recv,
    ctx_all,
    res_send,
    res_recv,
    extra,
    part,
    part_send,
    part_recv,
    attended,
    y_first,
    y_second,
    hid_all,
    acc,
    fin_send,
    fin_recv,
    in_sem,
    kv_sem,
    w_sem,
    ctx_ssem,
    ctx_rsem,
    res_ssem,
    res_rsem,
    part_ssem,
    part_rsem,
    z_ssem,
    z_rsem,
    y_ssem,
    y_rsem,
    c_ssem,
    c_rsem,
    hid_ssem,
    hid_rsem,
    fin_ssem,
    fin_rsem,
):
    me = lax.axis_index("dev")
    splits = n // COLS
    k = me // COLS
    c = lax.rem(me, COLS)
    rows = q_ref.shape[0]
    head_dim = keys.shape[2]
    cache_len = keys.shape[1]
    heads = q_ref.shape[1] // head_dim
    per_block = heads // splits
    db = wo.shape[1]
    half = db // HALVES
    ff = wg.shape[1]
    blk = rows * COLS
    all_rows = rows * n
    width = db * COLS
    y_all = (y_first, y_second)

    barrier = pltpu.get_barrier_semaphore()

    def loop(low, high, f):
        def step(i, carry):
            f(i)
            return carry

        lax.fori_loop(low, high, step, 0)

    def greet(i):
        pl.semaphore_signal(
            barrier,
            inc=1,
            device_id={"dev": lax.rem(me + i, n)},
            device_id_type=pl.DeviceIdType.MESH,
        )


    def remote(src, dst, ssem, rsem, dev):
        return pltpu.make_async_remote_copy(
            src_ref=src,
            dst_ref=dst,
            send_sem=ssem,
            recv_sem=rsem,
            device_id={"dev": dev},
            device_id_type=pl.DeviceIdType.MESH,
        )

    def xor(a, bits):
        bit = 1
        while bit <= bits:
            if bits & bit:
                a = a + bit - 2 * bit * lax.rem(a // bit, 2)
            bit *= 2
        return a

    beside = xor(c, 1)
    across = xor(c, 2)
    corner = xor(c, 3)
    plane = (c, beside, across, corner)

    small = [
        pltpu.make_async_copy(src, dst, in_sem.at[i])
        for i, (src, dst) in enumerate(
            (
                (q_hbm, q_ref),
                (len_hbm, len_ref),
                (res_hbm, res_ref),
                (gain_hbm, gain_ref),
                (ids_hbm, ids_ref),
                (score_hbm, score_ref),
            )
        )
    ]
    loads = [pltpu.make_async_copy(keys_hbm.at[r], keys.at[r], kv_sem.at[r]) for r in range(rows)]
    loads += [
        pltpu.make_async_copy(values_hbm.at[r], values.at[r], kv_sem.at[rows + r])
        for r in range(rows)
    ]
    load_o = pltpu.make_async_copy(wo_hbm.at[0], wo, w_sem.at[0])

    def span(i, size):
        return pl.ds(pl.multiple_of(plane[i] * size, size), size)

    load_g = [
        pltpu.make_async_copy(wg_hbm.at[span(i, db)], wg.at[span(i, db)], w_sem.at[1 + i])
        for i in range(COLS)
    ]
    load_u = [
        pltpu.make_async_copy(wu_hbm.at[span(i, db)], wu.at[span(i, db)], w_sem.at[5 + i])
        for i in range(COLS)
    ]
    load_d = [
        pltpu.make_async_copy(wd_hbm.at[0, span(i, ff)], wd.at[span(i, ff)], w_sem.at[9 + i])
        for i in range(COLS)
    ]
    small[0].start()
    small[1].start()
    for copy in loads:
        copy.start()
    for copy in small[2:]:
        copy.start()
    loop(1, n, greet)
    load_o.start()
    for i in range(COLS):
        load_g[i].start()
        load_u[i].start()
    for i in range(COLS):
        load_d[i].start()

    small[0].wait()
    small[1].wait()
    for h in range(heads):
        q_rows[h * rows : (h + 1) * rows, :] = q_ref[:, h * head_dim : (h + 1) * head_dim].astype(
            F32
        )
    qs = q_rows[...].astype(BF16)
    hr = heads * rows
    which = lax.rem(lax.broadcasted_iota(jnp.int32, (hr, 1), 0), rows)
    scores = jnp.zeros((hr, cache_len), F32)
    lengths = jnp.zeros((hr, 1), jnp.int32)
    for r in range(rows):
        loads[r].wait()
        s = lax.dot_general(qs, keys[r], (((1,), (1,)), ((), ())), preferred_element_type=F32)
        scores = jnp.where(which == r, s, scores)
        lengths = jnp.where(which == r, len_ref[r], lengths)
    live = lax.broadcasted_iota(jnp.int32, (hr, cache_len), 1) < lengths
    scores = jnp.where(live, scores * head_dim ** (-0.5), -1e30)
    largest = jnp.max(scores, axis=-1, keepdims=True)
    exponent = jnp.where(live, jnp.exp(scores - largest), 0.0)
    probs = exponent / jnp.sum(exponent, axis=-1, keepdims=True)
    context = jnp.zeros((hr, head_dim), F32)
    for r in range(rows):
        loads[rows + r].wait()
        context = context + dot(jnp.where(which == r, probs, 0.0).astype(BF16), values[r])
    for h in range(heads):
        b, at = h // per_block, h % per_block
        ctx_send[b, :, at * head_dim : (at + 1) * head_dim] = context[
            h * rows : (h + 1) * rows, :
        ].astype(BF16)

    for copy in small[2:]:
        copy.wait()
    shares = 1.0 / (1.0 + jnp.exp(-score_ref[...]))
    total = jnp.sum(shares, axis=-1, keepdims=True)
    lane = lax.broadcasted_iota(jnp.int32, (rows, LANES), 1)
    mine = jnp.zeros((rows, LANES), F32)
    for t in range(ids_ref.shape[1]):
        share = shares[:, t : t + 1] / total
        mine = mine + jnp.where(ids_ref[:, t : t + 1] + 2 == lane, share, 0.0)
    for j in range(COLS):
        res_send[j, :, 0:db] = res_ref[:, j * db : (j + 1) * db]
        res_send[j, :, db : db + LANES] = mine.astype(BF16)
    res_recv[c] = res_send[c]
    ctx_recv[me] = ctx_send[k]

    def ctx_copy(i):
        to = lax.rem(me + i, n)
        return remote(
            ctx_send.at[to // COLS], ctx_recv.at[me], ctx_ssem.at[i], ctx_rsem.at[i], to
        )

    def res_copy(i):
        to = lax.rem(c + i, COLS)
        return remote(
            res_send.at[to], res_recv.at[c], res_ssem.at[i], res_rsem.at[i], k * COLS + to
        )

    def part_copy(h, i):
        to = xor(k, i)
        return remote(
            part_send.at[h, to],
            part_recv.at[h, i],
            part_ssem.at[h, i],
            part_rsem.at[h, i],
            to * COLS + c,
        )

    pl.semaphore_wait(barrier, n - 1)
    loop(1, n, lambda i: ctx_copy(i).start())
    load_o.wait()
    loop(1, n, lambda i: ctx_copy(i).wait_recv())
    for d in range(n):
        ctx_all[d * rows : (d + 1) * rows, :] = ctx_recv[d].astype(F32)
    lhs = ctx_all[...].astype(BF16)

    for h in range(HALVES):
        cols = slice(h * half, (h + 1) * half)
        part[:, cols] = dot(lhs, wo[:, cols])
        for b in range(splits):
            part_send[h, b] = part[b * blk : (b + 1) * blk, cols].astype(BF16)
        for i in range(1, splits):
            part_copy(h, i).start()
        if h == 0:
            loop(1, COLS, lambda i: res_copy(i).start())

    loop(1, COLS, lambda i: res_copy(i).wait_recv())
    for j in range(COLS):
        attended[j * rows : (j + 1) * rows, :] = res_recv[j, :, 0:db].astype(F32)
        extra[j * rows : (j + 1) * rows, :] = res_recv[j, :, db : db + LANES].astype(F32)
    mine_rows = pl.ds(pl.multiple_of(k * blk, blk), blk)

    def piece(h, col, i):
        return y_all[h].at[col, pl.ds(pl.multiple_of(xor(k, i) * blk, blk), blk)]

    def z_copy(h, i):
        at = piece(h, c, 0)
        return remote(at, at, z_ssem.at[h, i], z_rsem.at[h, i], xor(k, i) * COLS + c)

    def y_copy(h, i):
        at = piece(h, c, i)
        return remote(at, at, y_ssem.at[h, i], y_rsem.at[h, i], k * COLS + across)

    def c_copy(h, far, i):
        at = piece(h, across if far else c, i)
        slot = splits * far + i
        return remote(at, at, c_ssem.at[h, slot], c_rsem.at[h, slot], k * COLS + beside)

    square = jnp.zeros((blk, 1), F32)
    for h in range(HALVES):
        cols = slice(h * half, (h + 1) * half)
        total = attended[:, cols] + part[mine_rows, cols]
        for i in range(1, splits):
            part_copy(h, i).wait_recv()
            total = total + part_recv[h, i].astype(F32)
        attended[:, cols] = total
        gain = gain_ref[:, pl.ds(pl.multiple_of(c * db + h * half, LANES), half)]
        square = square + jnp.sum(total * total, axis=-1, keepdims=True)
        y_all[h][c, mine_rows, 0:half] = (total * gain).astype(BF16)
        if h == HALVES - 1:
            high = square.astype(BF16).astype(F32)
            lane = lax.broadcasted_iota(jnp.int32, (blk, LANES), 1)
            packed = jnp.where(lane == 0, high, jnp.where(lane == 1, square - high, extra[...]))
            y_all[h][c, mine_rows, half : half + LANES] = packed.astype(BF16)
        for i in range(1, splits):
            z_copy(h, i).start()
        y_copy(h, 0).start()
        c_copy(h, 0, 0).start()

    def forward_z(h, i):
        z_copy(h, i).wait_recv()
        y_copy(h, i).start()
        c_copy(h, 0, i).start()

    def forward_y(h, i):
        y_copy(h, i).wait_recv()
        c_copy(h, 1, i).start()

    def chunk(h, i):
        if h == 0:
            load_g[i].wait()
            load_u[i].wait()
        lhs = y_all[h][plane[i], :, 0:half]
        at = pl.ds(pl.multiple_of(plane[i] * db + h * half, half), half)
        return dot(lhs, wg[at, :]), dot(lhs, wu[at, :])

    def arrive(h, far):
        for i in range(splits):
            c_copy(h, far, i).wait_recv()

    for i in range(1, splits):
        forward_z(0, i)
    gate, up = chunk(0, 0)
    forward_y(0, 0)
    for i in range(1, splits):
        forward_z(1, i)
        forward_y(0, i)
    arrive(0, 0)
    for h, i in ((0, 1), (1, 0), (0, 2)):
        g, u = chunk(h, i)
        gate, up = gate + g, up + u
    for i in range(splits):
        forward_y(1, i)
    arrive(0, 1)
    g, u = chunk(0, 3)
    gate, up = gate + g, up + u
    arrive(1, 0)
    for i in (1, 2):
        g, u = chunk(1, i)
        gate, up = gate + g, up + u
    arrive(1, 1)
    g, u = chunk(1, 3)
    gate, up = gate + g, up + u
    lane = lax.broadcasted_iota(jnp.int32, (all_rows, LANES), 1)
    square = jnp.zeros((all_rows, 1), F32)
    for j in range(COLS):
        tail = y_second[j, :, half : half + LANES].astype(F32)
        square = square + jnp.sum(jnp.where(lane < 2, tail, 0.0), axis=-1, keepdims=True)
    expert = k // (splits // EXPERTS)
    weight = jnp.sum(jnp.where(lane == expert + 2, tail, 0.0), axis=-1, keepdims=True)
    scale = lax.rsqrt(square * (1.0 / width) + 1e-5)
    gate = gate * scale
    hidden = gate / (1.0 + jnp.exp(-gate)) * (up * scale)
    hid_all[c] = hidden.astype(BF16)

    def hid_copy(i):
        at = hid_all.at[across if i == 3 else c]
        to = across if i == 2 else beside
        return remote(at, at, hid_ssem.at[i], hid_rsem.at[i], k * COLS + to)

    hid_copy(2).start()
    hid_copy(1).start()
    load_d[0].wait()
    acc[...] = dot(hid_all[c], wd[span(0, ff), :])
    load_d[1].wait()
    hid_copy(1).wait_recv()
    acc[...] += dot(hid_all[beside], wd[span(1, ff), :])
    hid_copy(2).wait_recv()
    hid_copy(3).start()
    load_d[2].wait()
    acc[...] += dot(hid_all[across], wd[span(2, ff), :])
    load_d[3].wait()
    hid_copy(3).wait_recv()

    def fin_copy(h, i):
        to = lax.rem(me + i, n)
        return remote(
            fin_send.at[h, to], fin_recv.at[h, me], fin_ssem.at[h, i], fin_rsem.at[h, i], to
        )

    for h in range(HALVES):
        cols = slice(h * half, (h + 1) * half)
        acc[:, cols] = (acc[:, cols] + dot(hid_all[corner], wd[span(3, ff), cols])) * weight
        acc[mine_rows, cols] = acc[mine_rows, cols] + attended[:, cols]
        for d in range(n):
            fin_send[h, d] = acc[d * rows : (d + 1) * rows, cols].astype(BF16)
        loop(1, n, lambda i: fin_copy(h, i).start())
        fin_recv[h, me] = fin_send[h, me]
    for h in range(HALVES):
        loop(1, n, lambda i: fin_copy(h, i).wait_recv())
        for j in range(COLS):
            total = fin_recv[h, j].astype(F32)
            for b in range(1, splits):
                total = total + fin_recv[h, b * COLS + j].astype(F32)
            out_ref[:, j * db + h * half : j * db + (h + 1) * half] = total.astype(BF16)

    loop(1, n, lambda i: ctx_copy(i).wait_send())
    loop(1, COLS, lambda i: res_copy(i).wait_send())
    for i in range(1, COLS):
        hid_copy(i).wait_send()
    for h in range(HALVES):
        loop(1, n, lambda i: fin_copy(h, i).wait_send())
        for i in range(splits):
            if i:
                part_copy(h, i).wait_send()
                z_copy(h, i).wait_send()
            y_copy(h, i).wait_send()
            c_copy(h, 0, i).wait_send()
            c_copy(h, 1, i).wait_send()


def body(
    queries,
    cache_keys,
    cache_values,
    row_lengths,
    residual,
    out_weight,
    norm_gain,
    expert_ids,
    gate_scores,
    gate_weight,
    up_weight,
    down_weight,
):
    n = lax.axis_size("dev")
    splits = n // COLS
    rows = queries.shape[0]
    head_dim = cache_keys.shape[2]
    heads = queries.shape[1] // head_dim
    kb, db = out_weight.shape[1:]
    ff = gate_weight.shape[1]
    all_rows = rows * n
    blk = rows * COLS
    half = db // HALVES
    vmem = pl.BlockSpec(memory_space=pltpu.VMEM)
    hbm = pl.BlockSpec(memory_space=pltpu.HBM)

    def dma(*count):
        return pltpu.SemaphoreType.DMA(count)

    return pl.pallas_call(
        functools.partial(kernel, n),
        out_shape=jax.ShapeDtypeStruct(residual.shape, BF16),
        in_specs=[hbm] * 12,
        out_specs=vmem,
        scratch_shapes=[
            pltpu.VMEM(queries.shape, BF16),
            pltpu.SMEM(row_lengths.shape, jnp.int32),
            pltpu.VMEM(residual.shape, BF16),
            pltpu.VMEM((1, norm_gain.shape[0]), F32),
            pltpu.VMEM(expert_ids.shape, jnp.int32),
            pltpu.VMEM(gate_scores.shape, F32),
            pltpu.VMEM(cache_keys.shape, BF16),
            pltpu.VMEM(cache_values.shape, BF16),
            pltpu.VMEM((kb, db), BF16),
            pltpu.VMEM(gate_weight.shape, BF16),
            pltpu.VMEM(up_weight.shape, BF16),
            pltpu.VMEM(down_weight.shape[1:], BF16),
            pltpu.VMEM((heads * rows, head_dim), F32),
            pltpu.VMEM((splits, rows, kb), BF16),
            pltpu.VMEM((n, rows, kb), BF16),
            pltpu.VMEM((all_rows, kb), F32),
            pltpu.VMEM((COLS, rows, db + LANES), BF16),
            pltpu.VMEM((COLS, rows, db + LANES), BF16),
            pltpu.VMEM((blk, LANES), F32),
            pltpu.VMEM((all_rows, db), F32),
            pltpu.VMEM((HALVES, splits, blk, half), BF16),
            pltpu.VMEM((HALVES, splits, blk, half), BF16),
            pltpu.VMEM((blk, db), F32),
            pltpu.VMEM((COLS, all_rows, half), BF16),
            pltpu.VMEM((COLS, all_rows, half + LANES), BF16),
            pltpu.VMEM((COLS, all_rows, ff), BF16),
            pltpu.VMEM((all_rows, db), F32),
            pltpu.VMEM((HALVES, n, rows, half), BF16),
            pltpu.VMEM((HALVES, n, rows, half), BF16),
            dma(6),
            dma(2 * rows),
            dma(13),
            dma(n),
            dma(n),
            dma(COLS),
            dma(COLS),
        ]
        + [dma(HALVES, splits)] * 6
        + [dma(HALVES, 2 * splits)] * 2
        + [dma(COLS)] * 2
        + [dma(HALVES, n)] * 2,
        compiler_params=pltpu.CompilerParams(
            collective_id=0, has_side_effects=True, vmem_limit_bytes=60 * 1024 * 1024
        ),
        name="layer",
    )(
        queries,
        row_lengths,
        residual,
        norm_gain[None, :],
        expert_ids,
        gate_scores,
        cache_keys,
        cache_values,
        out_weight,
        gate_weight,
        up_weight,
        down_weight,
    )


def solution(mesh):
    return jax.shard_map(
        body,
        mesh=mesh,
        in_specs=(
            P(("group", "dev"), None),
            P(("group", "dev"), None, None),
            P(("group", "dev"), None, None),
            P(("group", "dev")),
            P(("group", "dev"), None),
            P("dev", None, None),
            P(),
            P(("group", "dev"), None),
            P(("group", "dev"), None),
            P(None, "dev"),
            P(None, "dev"),
            P("dev", None, None),
        ),
        out_specs=P(("group", "dev"), None),
        check_vma=False,
    )
```
